512 devices in a mesh: pts: 64 (over x, z, core), ctr: 8 (over y).
Axes of the slice: x: 4, y: 8, z: 8, core: 2. Of those that a mesh axis runs over, the one named last changes fastest.
Arguments:
- points: bfloat16 [65536, 512], P('pts'), may hold values from -16 to 16
- centres: bfloat16 [16384, 512], P('ctr'), may hold values from -16 to 16
- vector: float32 [32, 16384], P(None, 'ctr'), may hold values from -6144 to 6144
- factor: float32 [16384, 16384], P('pts', 'ctr'), may hold values from -1 to 1, as said below
Outputs:
- update: float32 [32, 16384], P(None, 'ctr')
The draws below stay inside these ranges and needn't reach their ends.
Inputs may be any that keep to these rules, and one draw needn't show every extreme that they name: `factor`: entries below the diagonal blocks of 4096 by 4096 are zero.
All inputs are finite; a program needn't handle non-finite values.
Results may differ from the reference program's by a relative error of at most 0.0029.
Values sent between devices are 32-bit elements; how exact they have to be, the bound alone decides.
A program may use at most 64 MiB of HBM per device.

```python
import math
import jax
import jax.numpy as jnp
from jax import lax

D = 512
R = 32
PTS_DEV = 1024
NBLK = 4
POINTS = 65536
CENTRES = 16384
BLK = 4096
N_PTS = 64


def point_cloud(key):
    cluster_count = max(CENTRES // 64, 1)
    lane_width = 8
    mean_key = jax.random.fold_in(key, 101)
    noise_key = jax.random.fold_in(key, 103)
    label_key = jax.random.fold_in(key, 107)
    offset_key = jax.random.fold_in(key, 109)
    scale_key = jax.random.fold_in(key, 113)
    pick_key = jax.random.fold_in(key, 127)
    labels = jax.random.randint(label_key, (POINTS,), 0, cluster_count)
    offsets = jax.random.randint(offset_key, (cluster_count,), 0, D)
    means = jnp.clip(jax.random.normal(mean_key, (cluster_count, D), jnp.float32), -6.0, 6.0)
    noise = jnp.clip(jax.random.normal(noise_key, (POINTS, D), jnp.float32), -6.0, 6.0)
    scales = jnp.exp(jax.random.uniform(scale_key, (POINTS, 1), jnp.float32, math.log(0.7), math.log(1.4))) * (math.sqrt(D) / 8.0)
    coords = jnp.arange(D, dtype=jnp.int32)
    lanes = (coords[None, :] - offsets[:, None]) % D < lane_width
    row_means = jnp.take(means, labels, axis=0)
    row_lanes = jnp.take(lanes, labels, axis=0)
    values = row_means + jnp.where(row_lanes, scales * noise, 0.0)
    values = jnp.clip(values, -16.0, 16.0).astype(jnp.bfloat16)
    picked = jax.random.permutation(pick_key, POINTS)[:CENTRES]
    return (values, picked)


def draw_points(key, part):
    values, picked = point_cloud(jax.random.fold_in(key, 11))
    return values


def draw_centres(key, part):
    values, picked = point_cloud(jax.random.fold_in(key, 11))
    return jnp.take(values, picked, axis=0)


def draw_factor(key, part):
    value_key = jax.random.fold_in(key, 37)
    values = jax.random.normal(value_key, (CENTRES, CENTRES), jnp.float32)
    row_block = (jnp.arange(CENTRES) // BLK)[:, None]
    col_block = (jnp.arange(CENTRES) // BLK)[None, :]
    scaling = jnp.where(row_block == col_block, 2.0, jnp.where(row_block < col_block, 0.5, 0.0)) / math.sqrt(BLK)
    return jnp.clip(scaling * values, -1.0, 1.0)


def block_scale(stream_key, extent, split, low, top_value):
    loudness, own = 1.0, jax.random.fold_in(stream_key, 6)
    for dim, shards_of in split:
        heights = jnp.exp(jax.random.uniform(jax.random.fold_in(own, dim), (shards_of,), jnp.float32, low / len(split), top_value / len(split)))
        loudness = loudness * jnp.repeat(heights, extent[dim] // shards_of).reshape([-1 if axis == dim else 1 for axis in range(len(extent))])
    return loudness


def gaussian(stream_key, dims, spread, reach, split=(), held_as=jnp.bfloat16):
    result = jax.random.normal(stream_key, dims, jnp.float32) * spread
    if len(split) > 0:
        result = block_scale(stream_key, dims, split, -0.22, 0.18) * result
    return jnp.clip(result, min=-reach, max=reach).astype(held_as)


def setup_inputs(seed: int = 0) -> dict:
    splits = jax.random.split(jax.random.key(seed), 5)
    points = draw_points(jax.random.fold_in(splits[4], 71), 0)
    centres = draw_centres(jax.random.fold_in(splits[4], 71), 0)
    vector = gaussian(splits[2], (R, CENTRES), (CENTRES // 16), 6144.0, ((1, 8),), jnp.float32)
    factor = draw_factor(jax.random.fold_in(splits[4], 71), 0)
    return dict(points=points, centres=centres, vector=vector, factor=factor)


def kernel_tile(point_rows, centre_rows):
    inner_prods = lax.dot_general(point_rows, centre_rows, (((1,), (1,)), ((), ())), preferred_element_type=jnp.float32)
    point_norms = jnp.sum(jnp.square(point_rows.astype(jnp.float32)), axis=1)
    centre_norms = jnp.sum(jnp.square(centre_rows.astype(jnp.float32)), axis=1)
    distance = point_norms[:, None] + centre_norms[None, :] - 2.0 * inner_prods
    return jnp.exp(-(8.0 / D) * distance).astype(jnp.bfloat16)


def reference(points, centres, vector, factor):
    vector_low = vector.astype(jnp.bfloat16)
    grouped = points.reshape(N_PTS, PTS_DEV, D)

    def one_group(carry, point_rows):
        kernel = kernel_tile(point_rows, centres)
        images = lax.dot_general(vector_low, kernel, (((1,), (1,)), ((), ())), preferred_element_type=jnp.float32)
        images_low = (images / POINTS).astype(jnp.bfloat16)
        return carry + jnp.dot(images_low, kernel, preferred_element_type=jnp.float32), None

    total, _ = lax.scan(one_group, jnp.zeros((R, CENTRES), jnp.float32), grouped)
    update = jnp.zeros((R, CENTRES), jnp.float32)
    for block_idx in range(NBLK):
        lower = block_idx * BLK
        residual = total[:, lower:lower + BLK] - jnp.dot(update, factor[:, lower:lower + BLK], precision=lax.Precision.HIGHEST)
        solved = jnp.dot(residual, factor[lower:lower + BLK, lower:lower + BLK], precision=lax.Precision.HIGHEST)
        update = update.at[:, lower:lower + BLK].set(solved)
    return update
```

```python
import jax
import jax.numpy as jnp
from jax import lax
from jax.experimental import pallas as pl
from jax.experimental.pallas import tpu as pltpu
from jax.sharding import PartitionSpec as P

F32, BF16 = jnp.float32, jnp.bfloat16
MESH = pl.DeviceIdType.MESH
NN = (((1,), (0,)), ((), ()))
NT = (((1,), (1,)), ((), ()))
PT = 256
S_IR, S_IG, S_TC, S_FX, S_RT, S_X, S_G, S_RA, S_B, S_O1, S_O2, S_END = (
    0, 8, 16, 17, 18, 26, 27, 31, 39, 51, 55, 71)
(R_IR, R_IG, R_TC, R_FX, R_RT, R_X, R_IN, R_AB, R_O1, R_O2, L_C, L_P, L_V, R_END) = (
    0, 1, 2, 3, 4, 5, 6, 7, 11, 12, 13, 14, 15, 16)


def device(x, y, z, c):
    return ((x * 8 + z) * 2 + c, y)


def sweep_kernel(
    points, centres, vector, factor, out,
    pts, cen, vec, norm_row, kmat, fraw, fhigh, flow,
    im_src, im_rs, ag_src, im_ag, im_low, t_src, t_rc, rs_src, rs_t, x_src, x_buf,
    s_src, inp, ab_src, rs_ab, u_src, o_buf, ssem, rsem,
):
    p, y = lax.axis_index("pts"), lax.axis_index("ctr")
    x, z, c = p // 16, (p // 2) % 8, p % 2
    k, h = y // 2, y % 2
    diag, works, below = x == k, x <= k, x < k

    def send(src, dst, s, r, dev, own=None):
        def remote():
            pltpu.make_async_remote_copy(
                src_ref=src, dst_ref=dst, send_sem=ssem.at[s], recv_sem=rsem.at[r],
                device_id=dev, device_id_type=MESH).start()
        if own is None:
            remote()
        else:
            pl.when(jnp.logical_not(own))(remote)

            @pl.when(own)
            def _():
                pltpu.make_async_copy(src, dst, rsem.at[r]).start()

    def sent(src, s, dev, own=None):
        def finish():
            pltpu.make_async_remote_copy(
                src_ref=src, dst_ref=src, send_sem=ssem.at[s], recv_sem=rsem.at[0],
                device_id=dev, device_id_type=MESH).wait_send()
        if own is None:
            finish()
        else:
            pl.when(jnp.logical_not(own))(finish)

    def arrived(buf, r):
        pltpu.make_async_copy(buf, buf, rsem.at[r]).wait()

    def each(n, f):
        def step(i, carry):
            f(i)
            return carry
        lax.fori_loop(0, n, step, 0)

    load_c = pltpu.make_async_copy(centres, cen, rsem.at[L_C])
    load_p = pltpu.make_async_copy(points, pts, rsem.at[L_P])
    load_v = pltpu.make_async_copy(vector, vec, rsem.at[L_V])
    load_c.start()
    load_p.start()
    load_v.start()

    barrier = pltpu.get_barrier_semaphore()

    def greet(dev):
        pl.semaphore_signal(barrier, inc=1, device_id=dev, device_id_type=MESH)

    each(7, lambda i: greet(device(x, (y + 1 + i) % 8, z, c)))
    each(3, lambda i: greet(device(x, 2 * k + (h + (i + 1) // 2) % 2, z, (c + (i + 1) % 2) % 2)))
    rs_own = z // 2 == 2 * h + c
    rs_y, rs_c = 2 * k + z // 4, (z // 2) % 2

    def greet_rs(i):
        @pl.when(jnp.logical_not(rs_own & (i == z)))
        def _():
            greet(device(x, rs_y, i, rs_c))
    each(8, greet_rs)

    def greet_out(i):
        dev = (2 * k + i // 2 % 2, 4 * h + i // 4, i % 2)

        @pl.when(jnp.logical_not((dev[0] == y) & (dev[1] == z) & (dev[2] == c)))
        def _():
            greet(device(x, *dev))
    each(16, greet_out)
    out_own = z // 4 == h

    @pl.when(diag)
    def _():
        each(3, lambda i: greet(device((x + 1 + i) % 4, y, z, c)))
        each(8 * k, lambda i: greet(device(i // 8, rs_y, i % 8, rs_c)))

    @pl.when(jnp.logical_not(diag))
    def _():
        greet(device(k, y, z, c))

    @pl.when(below)
    def _():
        each(4, lambda i: greet(device(x, 2 * x + i // 2, z, i % 2)))

    load_c.wait()
    squares = jnp.square(cen[...].astype(F32))
    folded = (squares[:, 0:128] + squares[:, 128:256]) + (squares[:, 256:384] + squares[:, 384:512])
    norm_row[...] = jnp.sum(folded.T, axis=0, keepdims=True) * (1.0 / 64.0)
    load_p.wait()
    load_v.wait()

    def kernel_step(i):
        rows = pl.ds(pl.multiple_of(i * PT, PT), PT)
        pt = pts[rows, :]
        prods = lax.dot_general(pt, cen[...], NT, preferred_element_type=F32)
        norms = jnp.sum(jnp.square(pt.astype(F32)), axis=1, keepdims=True) * (1.0 / 64.0)
        kern = jnp.exp(prods * (1.0 / 32.0) - (norms + norm_row[...])).astype(BF16)
        kmat[rows, :] = kern
        images = lax.dot_general(vec[...].astype(BF16), kern, NT, preferred_element_type=F32)
        im_src[2 * i] = images[:, 0:128]
        im_src[2 * i + 1] = images[:, 128:256]
    each(4, kernel_step)

    own_count = jnp.where(rs_own, 1, 0) + jnp.where(out_own, 1, 0)
    place_count = jnp.where(diag, 3 + 4 * (3 - k), 1) + jnp.where(below, 8, 0)
    pl.semaphore_wait(barrier, 7 + 3 + 8 + 16 - own_count + place_count)

    each(8, lambda i: send(im_src.at[i], im_rs.at[y], S_IR + i, R_IR, device(x, i, z, c), i == y))

    my_rows = pl.ds(pl.multiple_of(c * 256, 256), 256)
    keep = pl.ds(pl.multiple_of(c * 1024, 1024), 1024)
    give = pl.ds(pl.multiple_of((1 - c) * 1024, 1024), 1024)
    partner = device(x, y, z, 1 - c)

    @pl.when(works)
    def _():
        send(factor.at[:, give], fraw.at[my_rows, :], S_FX, R_FX, partner)
        pltpu.make_async_copy(factor.at[:, keep], fraw.at[my_rows, :], rsem.at[R_FX]).start()

    arrived(im_rs, R_IR)
    total = ((im_rs[0] + im_rs[1]) + (im_rs[2] + im_rs[3])) + (
        (im_rs[4] + im_rs[5]) + (im_rs[6] + im_rs[7]))
    ag_src[...] = (total / 65536.0).astype(BF16).astype(F32)
    each(8, lambda i: send(ag_src, im_ag.at[y], S_IG + i, R_IG, device(x, i, z, c), i == y))

    @pl.when(works)
    def _():
        arrived(fraw, R_FX)
        raw = fraw[...]
        high = raw.astype(BF16)
        fhigh[...] = high
        flow[...] = (raw - high.astype(F32)).astype(BF16)

    arrived(im_ag, R_IG)
    for i in range(8):
        im_low[:, i * 128:(i + 1) * 128] = im_ag[i].astype(BF16)

    t_src[...] = lax.dot_general(im_low[...], kmat[:, give], NN, preferred_element_type=F32)
    send(t_src, t_rc, S_TC, R_TC, partner)
    mine = lax.dot_general(im_low[...], kmat[:, keep], NN, preferred_element_type=F32)
    arrived(t_rc, R_TC)
    mine = mine + t_rc[...]
    for i in range(8):
        rs_src[i] = mine[:, i * 128:(i + 1) * 128]

    def piece_dev(i, to):
        zt, ht, ct = 4 * h + 2 * c + i // 4, i // 2 % 2, i % 2
        own = (to == x) & (zt == z) & (ht == h) & (ct == c)
        return device(to, 2 * k + ht, zt, ct), own

    def scatter(src, dst, s, r, to):
        def one(i):
            dev, own = piece_dev(i, to)
            send(src.at[i], dst, s + i, r, dev, own)
        each(8, one)

    def eight(buf, *lead):
        v = [buf[(*lead, i)] for i in range(8)]
        return ((v[0] + v[1]) + (v[2] + v[3])) + ((v[4] + v[5]) + (v[6] + v[7]))

    scatter(rs_src, rs_t.at[z], S_RT, R_RT, x)
    arrived(rs_t, R_RT)
    x_src[...] = eight(rs_t)

    @pl.when(jnp.logical_not(diag))
    def _():
        send(x_src, x_buf.at[(x - k + 3) % 4], S_X, R_X, device(k, y, z, c))

    def slab_dev(i):
        own = (i // 2 == h) & (i % 2 == c)
        return device(x, 2 * k + i // 2, z, i % 2), own

    @pl.when(diag)
    def _():
        arrived(x_buf, R_X)
        s_src[...] = (x_src[...] + x_buf[0]) + (x_buf[1] + x_buf[2])
        for j in range(3):
            @pl.when(j < k)
            def _():
                arrived(rs_ab.at[j], R_AB + j)
                s_src[...] -= eight(rs_ab, j)
        each(4, lambda i: send(s_src, inp.at[2 * h + c], S_G + i, R_IN, *slab_dev(i)))

    @pl.when(works)
    def _():
        arrived(inp, R_IN)
        v = jnp.concatenate([inp[i] for i in range(4)], axis=1)
        high = v.astype(BF16)
        both = jnp.concatenate([high, (v - high.astype(F32)).astype(BF16)], axis=0)
        prod = lax.dot_general(both, fhigh[...], NN, preferred_element_type=F32)
        rest = lax.dot_general(high, flow[...], NN, preferred_element_type=F32)
        part = prod[0:32] + (prod[32:64] + rest)
        for i in range(8):
            ab_src[i] = part[:, i * 128:(i + 1) * 128]
        scatter(ab_src, rs_ab.at[x, z], S_RA, R_AB + x, k)

    def later_dev(i):
        return device(x, 2 * (k + 1) + i // 2, z, i % 2)

    @pl.when(diag)
    def _():
        arrived(rs_ab.at[k], R_AB + k)
        u_src[...] = eight(rs_ab, k)
        each(4 * (3 - k), lambda i: send(u_src, inp.at[2 * h + c], S_B + i, R_IN, later_dev(i)))
        each(3, lambda i: send(u_src, u_src, S_O1 + i, R_O1, device((x + 1 + i) % 4, y, z, c)))

    @pl.when(jnp.logical_not(diag))
    def _():
        arrived(u_src, R_O1)

    def out_dev(i):
        own = out_own & (i // 2 == z) & (i % 2 == c)
        return device(x, 2 * k + z // 4, i // 2, i % 2), own

    slot = (z % 4) * 4 + 2 * h + c
    each(16, lambda i: send(u_src, o_buf.at[slot], S_O2 + i, R_O2, *out_dev(i)))
    arrived(o_buf, R_O2)
    for i in range(16):
        out[:, i * 128:(i + 1) * 128] = o_buf[i]

    each(8, lambda i: sent(im_src.at[i], S_IR + i, device(x, i, z, c), i == y))
    each(8, lambda i: sent(ag_src, S_IG + i, device(x, i, z, c), i == y))
    sent(t_src, S_TC, partner)

    def scattered(src, s, to):
        def one(i):
            dev, own = piece_dev(i, to)
            sent(src.at[i], s + i, dev, own)
        each(8, one)
    scattered(rs_src, S_RT, x)

    @pl.when(works)
    def _():
        sent(factor.at[:, give], S_FX, partner)
        scattered(ab_src, S_RA, k)

    @pl.when(jnp.logical_not(diag))
    def _():
        sent(x_src, S_X, device(k, y, z, c))

    @pl.when(diag)
    def _():
        each(4, lambda i: sent(s_src, S_G + i, *slab_dev(i)))
        each(4 * (3 - k), lambda i: sent(u_src, S_B + i, later_dev(i)))
        each(3, lambda i: sent(u_src, S_O1 + i, device((x + 1 + i) % 4, y, z, c)))
    each(16, lambda i: sent(u_src, S_O2 + i, *out_dev(i)))


def body(points, centres, vector, factor):
    def piece(*lead):
        return pltpu.VMEM((*lead, 32, 128), F32)

    any_space = pl.BlockSpec(memory_space=pl.ANY)
    return pl.pallas_call(
        sweep_kernel,
        out_shape=jax.ShapeDtypeStruct((32, 2048), F32),
        in_specs=[any_space] * 4,
        out_specs=pl.BlockSpec(memory_space=pltpu.VMEM),
        scratch_shapes=[
            pltpu.VMEM((1024, 512), BF16), pltpu.VMEM((2048, 512), BF16), pltpu.VMEM((32, 2048), F32),
            pltpu.VMEM((1, 2048), F32), pltpu.VMEM((1024, 2048), BF16),
            pltpu.VMEM((512, 1024), F32), pltpu.VMEM((512, 1024), BF16), pltpu.VMEM((512, 1024), BF16),
            piece(8), piece(8), piece(), piece(8), pltpu.VMEM((32, 1024), BF16),
            pltpu.VMEM((32, 1024), F32), pltpu.VMEM((32, 1024), F32), piece(8), piece(8), piece(), piece(3),
            piece(), piece(4), piece(8), piece(4, 8), piece(), piece(16),
            pltpu.SemaphoreType.DMA((S_END,)), pltpu.SemaphoreType.DMA((R_END,)),
        ],
        compiler_params=pltpu.CompilerParams(
            collective_id=0, has_side_effects=True, vmem_limit_bytes=48 * 2**20),
        cost_estimate=pl.CostEstimate(
            flops=2 * 1024 * 2048 * 512, bytes_accessed=6 * 2**20, transcendentals=1024 * 2048),
    )(points, centres, vector, factor)


def solution(mesh):
    placed = (P("pts", None), P("ctr", None), P(None, "ctr"), P("pts", "ctr"))
    return jax.shard_map(
        body, mesh=mesh, in_specs=placed, out_specs=P(None, "ctr"), check_vma=False
    )
```

```python
import jax
import jax.numpy as jnp
from jax import lax
from jax.experimental import pallas as pl
from jax.experimental.pallas import tpu as pltpu
from jax.sharding import PartitionSpec as P

F32, BF16 = jnp.float32, jnp.bfloat16
MESH = pl.DeviceIdType.MESH
NN = (((1,), (0,)), ((), ()))
NT = (((1,), (1,)), ((), ()))
PT = 256
AROUND = (4, 3, 5, 2, 6, 1, 7)
S_IR, S_IG, S_TC, S_FX, S_RT, S_X, S_G, S_RA, S_B, S_O1, S_O2, S_O3, S_END = (
    0, 8, 16, 17, 18, 26, 27, 31, 39, 51, 55, 71, 72)
(R_IR, R_IG, R_TC, R_FX, R_RT, R_X, R_IN, R_AB, R_O1, R_O2, R_O3, L_C, L_P, L_V, R_END) = (
    0, 1, 2, 3, 4, 5, 6, 7, 11, 12, 13, 14, 15, 16, 17)


def device(x, y, z, c):
    return ((x * 8 + z) * 2 + c, y)


def sweep_kernel(
    points, centres, vector, factor, out,
    pts, cen, vec, norm_row, kmat, fraw, fhigh, flow,
    im_src, im_rs, ag_src, im_ag, im_low, t_src, t_rc, rs_src, rs_t, x_src, x_buf,
    s_src, inp, ab_src, rs_ab, u_src, o_buf, ssem, rsem,
):
    p, y = lax.axis_index("pts"), lax.axis_index("ctr")
    x, z, c = p // 16, (p // 2) % 8, p % 2
    k, h = y // 2, y % 2
    diag, works, below, last = x == k, x <= k, x < k, k == 3

    pending = []

    def send(src, dst, s, r, dev, when=None, like=None):
        def start():
            pltpu.make_async_remote_copy(
                src_ref=src, dst_ref=dst, send_sem=ssem.at[s], recv_sem=rsem.at[r],
                device_id=dev, device_id_type=MESH).start()

        def sent():
            buf = src if like is None else like()
            pltpu.make_async_copy(buf, buf, ssem.at[s]).wait()
        if when is None:
            start()
            pending.append(sent)
        else:
            pl.when(when)(start)
            pending.append(lambda: pl.when(when)(sent))

    def nested(first, when):
        inner = pending[first:]
        del pending[first:]

        def waits():
            for wait in inner:
                wait()
        pending.append(lambda: pl.when(when)(waits))

    def stay(src, dst, r):
        pltpu.make_async_copy(src, dst, rsem.at[r]).start()

    def arrived(buf, r):
        pltpu.make_async_copy(buf, buf, rsem.at[r]).wait()

    def each(n, f):
        def step(i, carry):
            f(i)
            return carry
        lax.fori_loop(0, n, step, 0)

    load_c = pltpu.make_async_copy(centres, cen, rsem.at[L_C])
    load_p = pltpu.make_async_copy(points, pts, rsem.at[L_P])
    load_v = pltpu.make_async_copy(vector, vec, rsem.at[L_V])
    load_c.start()
    load_p.start()
    load_v.start()

    barrier = pltpu.get_barrier_semaphore()

    def greet(dev):
        pl.semaphore_signal(barrier, inc=1, device_id=dev, device_id_type=MESH)

    each(7, lambda i: greet(device(x, (y + 1 + i) % 8, z, c)))
    each(3, lambda i: greet(device(x, 2 * k + (h + (i + 1) // 2) % 2, z, (c + (i + 1) % 2) % 2)))
    rs_own = z // 2 == 2 * h + c
    rs_y, rs_c = 2 * k + z // 4, (z // 2) % 2

    def greet_rs(i):
        @pl.when(jnp.logical_not(rs_own & (i == z)))
        def _():
            greet(device(x, rs_y, i, rs_c))
    each(8, greet_rs)

    def greet_out(i):
        dev = (2 * k + i // 2 % 2, 4 * h + i // 4, i % 2)

        @pl.when(jnp.logical_not((dev[0] == y) & (dev[1] == z) & (dev[2] == c)))
        def _():
            greet(device(x, *dev))
    pl.when(jnp.logical_not(last))(lambda: each(16, greet_out))
    pl.when(last)(lambda: each(7, lambda i: greet(device(x, y, (z + 1 + i) % 8, c))))
    out_own = z // 4 == h
    rs_away, out_away = jnp.logical_not(rs_own), jnp.logical_not(out_own)
    off_diag, not_last = jnp.logical_not(diag), jnp.logical_not(last)
    plain = diag & last
    dealt = works & jnp.logical_not(plain)
    ab_own = rs_own & diag
    ab_away = jnp.logical_not(ab_own)
    more = [k + 1 + j <= 3 for j in range(3)]

    @pl.when(diag)
    def _():
        each(3, lambda i: greet(device((x + 1 + i) % 4, y, z, c)))
        each(8 * k, lambda i: greet(device(i // 8, rs_y, i % 8, rs_c)))

    @pl.when(jnp.logical_not(diag))
    def _():
        greet(device(k, y, z, c))

    @pl.when(below)
    def _():
        each(4, lambda i: greet(device(x, 2 * x + i // 2, z, i % 2)))

    load_c.wait()
    squares = jnp.square(cen[...].astype(F32))
    folded = (squares[:, 0:128] + squares[:, 128:256]) + (squares[:, 256:384] + squares[:, 384:512])
    norm_row[...] = jnp.sum(folded.T, axis=0, keepdims=True) * (1.0 / 64.0)
    load_p.wait()
    load_v.wait()

    def kernel_step(i):
        rows = pl.ds(pl.multiple_of(i * PT, PT), PT)
        pt = pts[rows, :]
        prods = lax.dot_general(pt, cen[...], NT, preferred_element_type=F32)
        norms = jnp.sum(jnp.square(pt.astype(F32)), axis=1, keepdims=True) * (1.0 / 64.0)
        kern = jnp.exp(prods * (1.0 / 32.0) - (norms + norm_row[...])).astype(BF16)
        kmat[rows, :] = kern
        images = lax.dot_general(vec[...].astype(BF16), kern, NT, preferred_element_type=F32)
        im_src[2 * i] = images[:, 0:128]
        im_src[2 * i + 1] = images[:, 128:256]
    each(4, kernel_step)

    scatter_count = 8 - jnp.where(rs_own, 1, 0)
    result_count = jnp.where(last, 7, 16 - jnp.where(out_own, 1, 0))
    place_count = jnp.where(diag, 3 + 4 * (3 - k), 1) + jnp.where(below, 8, 0)
    pl.semaphore_wait(barrier, 7 + 3 + scatter_count + result_count + place_count)

    def phase_images():
        for n, d in enumerate(AROUND):
            i = (y + d) % 8
            send(im_src.at[i], im_rs.at[y], S_IR + n, R_IR, device(x, i, z, c), like=lambda: im_src.at[0])
        stay(im_src.at[y], im_rs.at[y], R_IR)

    my_rows = pl.ds(pl.multiple_of(c * 256, 256), 256)
    keep = pl.ds(pl.multiple_of(c * 1024, 1024), 1024)
    give = pl.ds(pl.multiple_of((1 - c) * 1024, 1024), 1024)
    partner = device(x, y, z, 1 - c)

    def phase_factor():
        send(factor.at[:, give], fraw.at[my_rows, :], S_FX, R_FX, partner, works, lambda: fraw.at[0:256, :])

        @pl.when(works)
        def _():
            stay(factor.at[:, keep], fraw.at[my_rows, :], R_FX)

    def phase_split():
        @pl.when(works)
        def _():
            arrived(fraw, R_FX)
            raw = fraw[...]
            high = raw.astype(BF16)
            fhigh[...] = high
            flow[...] = (raw - high.astype(F32)).astype(BF16)

    def eight(buf, *lead):
        v = [buf[(*lead, i)] for i in range(8)]
        return ((v[0] + v[1]) + (v[2] + v[3])) + ((v[4] + v[5]) + (v[6] + v[7]))

    def phase_rounded():
        arrived(im_rs, R_IR)
        ag_src[...] = (eight(im_rs) / 65536.0).astype(BF16).astype(F32)
        for n, d in enumerate(AROUND):
            send(ag_src, im_ag.at[y], S_IG + n, R_IG, device(x, (y + d) % 8, z, c))
        stay(ag_src, im_ag.at[y], R_IG)

        arrived(im_ag, R_IG)
        for i in range(8):
            im_low[:, i * 128:(i + 1) * 128] = im_ag[i].astype(BF16)

    def piece(b):
        zb, hb, cb = (z + b // 4) % 2, (h + b // 2 % 2) % 2, (c + b % 2) % 2
        return 4 * zb + 2 * hb + cb, (2 * k + hb, 4 * h + 2 * c + zb, cb)

    def scatter(src, dst, s, r, to, own, away, bits):
        for b in bits:
            g, place = piece(b)
            send(src.at[g], dst, s + b, r, device(to, *place), None if b else away, lambda: src.at[0])
            if not b:
                pl.when(own)(lambda: stay(src.at[g], dst, r))

    def phase_totals():
        t_src[...] = lax.dot_general(im_low[...], kmat[:, give], NN, preferred_element_type=F32)
        send(t_src, t_rc, S_TC, R_TC, partner)
        mine = lax.dot_general(im_low[...], kmat[:, keep], NN, preferred_element_type=F32)
        arrived(t_rc, R_TC)
        mine = mine + t_rc[...]
        for i in range(8):
            rs_src[i] = mine[:, i * 128:(i + 1) * 128]
        scatter(rs_src, rs_t.at[z], S_RT, R_RT, x, rs_own, rs_away, (7, 6, 5, 4, 3, 2, 1, 0))

    def phase_across():
        arrived(rs_t, R_RT)
        x_src[...] = eight(rs_t)
        send(x_src, x_buf.at[(x - k + 3) % 4], S_X, R_X, device(k, y, z, c), off_diag)

    def phase_residual():
        @pl.when(diag)
        def _():
            first = len(pending)
            arrived(x_buf, R_X)
            s_src[...] = (x_src[...] + x_buf[0]) + (x_buf[1] + x_buf[2])
            for j in range(3):
                @pl.when(j < k)
                def _():
                    arrived(rs_ab.at[j], R_AB + j)
                    s_src[...] -= eight(rs_ab, j)
            for n in (3, 2, 1):
                send(s_src, inp.at[2 * h + c], S_G + n, R_IN,
                     device(x, 2 * k + (h + n // 2) % 2, z, (c + n % 2) % 2))
            stay(s_src, inp.at[2 * h + c], R_IN)
            nested(first, diag)

    def phase_product():
        @pl.when(works)
        def _():
            first = len(pending)
            arrived(inp, R_IN)
            v = jnp.concatenate([inp[i] for i in range(4)], axis=1)
            high = v.astype(BF16)
            both = jnp.concatenate([high, (v - high.astype(F32)).astype(BF16)], axis=0)
            far = jnp.where(plain, (z // 4 + 1) % 2, (z + 1) % 2) * 4
            for own_half in range(2):
                start = far + own_half * (4 - 2 * far)
                cols = pl.ds(pl.multiple_of(start * 128, 512), 512)
                prod = lax.dot_general(both, fhigh[:, cols], NN, preferred_element_type=F32)
                rest = lax.dot_general(high, flow[:, cols], NN, preferred_element_type=F32)
                part = prod[0:32] + (prod[32:64] + rest)
                for i in range(4):
                    ab_src[start + i] = part[:, i * 128:(i + 1) * 128]

                @pl.when(plain)
                def _():
                    inside = len(pending)
                    for n in range(4):
                        g = start + (z + 2 + n) % 4
                        if own_half and n == 2:
                            stay(ab_src.at[g], rs_ab.at[x, z], R_AB + x)
                        else:
                            send(ab_src.at[g], rs_ab.at[x, z], S_RA + 4 * own_half + n, R_AB + x,
                                 device(x, y, g, c), None, lambda: ab_src.at[0])
                    nested(inside, plain)

                @pl.when(dealt)
                def _():
                    inside = len(pending)
                    bits = (3, 2, 1, 0) if own_half else (7, 6, 5, 4)
                    scatter(ab_src, rs_ab.at[x, z], S_RA, R_AB + x, k, ab_own, ab_away, bits)
                    nested(inside, dealt)
            nested(first, works)

    def phase_solved():
        @pl.when(diag)
        def _():
            first = len(pending)
            arrived(rs_ab.at[k], R_AB + k)
            u_src[...] = eight(rs_ab, k)
            for j in range(3):
                for n in range(4):
                    send(u_src, inp.at[2 * h + c], S_B + 4 * j + n, R_IN,
                         device(x, (2 * (k + 1 + j) + n // 2) % 8, z, n % 2), more[j])
            for n in range(3):
                send(u_src, u_src, S_O1 + n, R_O1, device((x + 1 + n) % 4, y, z, c))
            nested(first, diag)

        @pl.when(jnp.logical_not(diag))
        def _():
            arrived(u_src, R_O1)

    def phase_results():
        @pl.when(not_last)
        def _():
            first = len(pending)
            slot = (z % 4) * 4 + 2 * h + c
            for n, d in enumerate(AROUND):
                for e in range(2):
                    zt = (z + d) % 8
                    send(u_src, o_buf.at[slot], S_O2 + 2 * n + e, R_O2, device(x, 2 * k + z // 4, zt, (c + e) % 2))
            send(u_src, o_buf.at[slot], S_O2 + 14, R_O2, device(x, 2 * k + z // 4, z, 1 - c))
            send(u_src, o_buf.at[slot], S_O2 + 15, R_O2, device(x, 2 * k + z // 4, z, c), out_away)

            @pl.when(out_own)
            def _():
                stay(u_src, o_buf.at[slot], R_O2)
            arrived(o_buf, R_O2)
            nested(first, not_last)

        @pl.when(last)
        def _():
            first = len(pending)
            slot = c * 8 + z
            for n, d in enumerate(AROUND):
                send(u_src, o_buf.at[slot], S_O2 + n, R_O2, device(x, y, (z + d) % 8, c))
            stay(u_src, o_buf.at[slot], R_O2)
            mine = o_buf.at[pl.ds(c * 8, 8)]
            arrived(mine, R_O2)
            send(mine, mine, S_O3, R_O3, partner, None, lambda: o_buf.at[0:8])
            arrived(o_buf.at[pl.ds(8 - c * 8, 8)], R_O3)
            nested(first, last)
        for i in range(16):
            out[:, i * 128:(i + 1) * 128] = o_buf[i]

    phases = (phase_images, phase_factor, phase_rounded, phase_totals, phase_across, phase_split, phase_residual,
              phase_product, phase_solved, phase_results)
    for phase in phases:
        phase()
    for wait in pending:
        wait()


def body(points, centres, vector, factor):
    def piece(*lead):
        return pltpu.VMEM((*lead, 32, 128), F32)

    any_space = pl.BlockSpec(memory_space=pl.ANY)
    return pl.pallas_call(
        sweep_kernel,
        out_shape=jax.ShapeDtypeStruct((32, 2048), F32),
        in_specs=[any_space] * 4,
        out_specs=pl.BlockSpec(memory_space=pltpu.VMEM),
        scratch_shapes=[
            pltpu.VMEM((1024, 512), BF16), pltpu.VMEM((2048, 512), BF16), pltpu.VMEM((32, 2048), F32),
            pltpu.VMEM((1, 2048), F32), pltpu.VMEM((1024, 2048), BF16),
            pltpu.VMEM((512, 1024), F32), pltpu.VMEM((512, 1024), BF16), pltpu.VMEM((512, 1024), BF16),
            piece(8), piece(8), piece(), piece(8), pltpu.VMEM((32, 1024), BF16),
            pltpu.VMEM((32, 1024), F32), pltpu.VMEM((32, 1024), F32), piece(8), piece(8), piece(), piece(3),
            piece(), piece(4), piece(8), piece(4, 8), piece(), piece(16),
            pltpu.SemaphoreType.DMA((S_END,)), pltpu.SemaphoreType.DMA((R_END,)),
        ],
        compiler_params=pltpu.CompilerParams(
            collective_id=0, has_side_effects=True, vmem_limit_bytes=60 * 2**20),
        cost_estimate=pl.CostEstimate(
            flops=2 * 1024 * 2048 * 512, bytes_accessed=6 * 2**20, transcendentals=1024 * 2048),
    )(points, centres, vector, factor)


def solution(mesh):
    placed = (P("pts", None), P("ctr", None), P(None, "ctr"), P("pts", "ctr"))
    return jax.shard_map(
        body, mesh=mesh, in_specs=placed, out_specs=P(None, "ctr"), check_vma=False
    )
```

```python
import jax
import jax.numpy as jnp
from jax import lax
from jax.experimental import pallas as pl
from jax.experimental.pallas import tpu as pltpu
from jax.sharding import PartitionSpec as P

F32, BF16 = jnp.float32, jnp.bfloat16
MESH = pl.DeviceIdType.MESH
NN = (((1,), (0,)), ((), ()))
NT = (((1,), (1,)), ((), ()))
PT = 256
AROUND = (4, 3, 5, 2, 6, 1, 7)
S_IR, S_IG, S_TC, S_FX, S_RT, S_X, S_G, S_RA, S_B, S_O1, S_O2, S_O3, S_END = (
    0, 14, 28, 29, 30, 38, 42, 46, 54, 66, 70, 86, 87)
(R_IR, R_IG, R_TC, R_FX, R_RT, R_X, R_IN, R_AB, R_O1, R_O2, R_O3, R_XQ, L_C, L_P, L_V, L_O, R_END) = (
    0, 2, 4, 5, 6, 7, 8, 9, 13, 14, 15, 16, 17, 18, 19, 20, 21)


def device(x, y, z, c):
    return ((x * 8 + z) * 2 + c, y)


def sweep_kernel(
    points, centres, vector, factor, out,
    pts, cen, vec, vec_low, norm_row, kmat, fraw, fhigh, flow,
    im_src, im_rs, ag_src, im_ag, im_low, t_keep, t_src, t_rc, rs_src, rs_t, x_src, x_buf,
    s_src, inp, ab_src, rs_ab, u_src, o_buf, x_quad, out_vm, ssem, rsem,
):
    p, y = lax.axis_index("pts"), lax.axis_index("ctr")
    x, z, c = p // 16, (p // 2) % 8, p % 2
    k, h = y // 2, y % 2
    diag, works, below, last = x == k, x <= k, x < k, k == 3
    first_pair = k == 0

    pending = []

    def send(src, dst, s, r, dev, when=None, like=None):
        def start():
            pltpu.make_async_remote_copy(
                src_ref=src, dst_ref=dst, send_sem=ssem.at[s], recv_sem=rsem.at[r],
                device_id=dev, device_id_type=MESH).start()

        def sent():
            buf = src if like is None else like()
            pltpu.make_async_copy(buf, buf, ssem.at[s]).wait()
        if when is None:
            start()
            pending.append(sent)
        else:
            pl.when(when)(start)
            pending.append(lambda: pl.when(when)(sent))

    def nested(first, when):
        inner = pending[first:]
        del pending[first:]

        def waits():
            for wait in inner:
                wait()
        pending.append(lambda: pl.when(when)(waits))

    def stay(src, dst, r):
        pltpu.make_async_copy(src, dst, rsem.at[r]).start()

    def arrived(buf, r):
        pltpu.make_async_copy(buf, buf, rsem.at[r]).wait()

    def each(n, f):
        def step(i, carry):
            f(i)
            return carry
        lax.fori_loop(0, n, step, 0)

    load_c = pltpu.make_async_copy(centres, cen, rsem.at[L_C])
    load_p = pltpu.make_async_copy(points, pts, rsem.at[L_P])
    load_v = pltpu.make_async_copy(vector, vec, rsem.at[L_V])
    load_c.start()
    load_p.start()
    load_v.start()

    barrier = pltpu.get_barrier_semaphore()

    def greet(dev):
        pl.semaphore_signal(barrier, inc=1, device_id=dev, device_id_type=MESH)

    each(7, lambda i: greet(device(x, (y + 1 + i) % 8, z, c)))
    each(3, lambda i: greet(device(x, 2 * k + (h + (i + 1) // 2) % 2, z, (c + (i + 1) % 2) % 2)))
    rs_own = z // 2 == 2 * h + c
    rs_y, rs_c = 2 * k + z // 4, (z // 2) % 2

    def greet_rs(i):
        @pl.when(jnp.logical_not(rs_own & (i == z)))
        def _():
            greet(device(x, rs_y, i, rs_c))
    each(8, greet_rs)

    def greet_out(i):
        dev = (2 * k + i // 2 % 2, 4 * h + i // 4, i % 2)

        @pl.when(jnp.logical_not((dev[0] == y) & (dev[1] == z) & (dev[2] == c)))
        def _():
            greet(device(x, *dev))
    pl.when(jnp.logical_not(last))(lambda: each(16, greet_out))
    pl.when(last)(lambda: each(7, lambda i: greet(device(x, y, (z + 1 + i) % 8, c))))
    out_own = z // 4 == h
    later_pair = jnp.logical_not(first_pair)
    fed = jnp.logical_not(diag & first_pair)
    later_diag = diag & later_pair
    rs_away, out_away = jnp.logical_not(rs_own), jnp.logical_not(out_own)
    off_diag, not_last = jnp.logical_not(diag), jnp.logical_not(last)
    plain = diag & last
    dealt = works & jnp.logical_not(plain)
    ab_own = rs_own & diag
    ab_away = jnp.logical_not(ab_own)
    more = [k + 1 + j <= 3 for j in range(3)]

    @pl.when(diag)
    def _():
        @pl.when(first_pair)
        def _():
            each(12, lambda i: greet(device(1 + i // 4, i // 2 % 2, z, i % 2)))

        @pl.when(jnp.logical_not(first_pair))
        def _():
            each(3, lambda i: greet(device((x + 1 + i) % 4, y, z, c)))
        each(8 * k, lambda i: greet(device(i // 8, rs_y, i % 8, rs_c)))

    @pl.when(jnp.logical_not(diag))
    def _():
        greet(device(k, y, z, c))

    @pl.when(below)
    def _():
        each(4, lambda i: greet(device(x, 2 * x + i // 2, z, i % 2)))

    load_c.wait()
    squares = jnp.square(cen[...].astype(F32))
    folded = (squares[:, 0:128] + squares[:, 128:256]) + (squares[:, 256:384] + squares[:, 384:512])
    norm_row[...] = jnp.sum(folded.T, axis=0, keepdims=True) * (1.0 / 64.0)
    load_p.wait()
    load_v.wait()
    vec_low[...] = vec[...].astype(BF16)

    def kernel_step(i):
        rows = pl.ds(i * PT, PT)
        pt = pts[rows, :]
        prods = lax.dot_general(pt, cen[...], NT, preferred_element_type=F32)
        norms = jnp.sum(jnp.square(pt.astype(F32)), axis=1, keepdims=True) * (1.0 / 64.0)
        kern = jnp.exp(prods * (1.0 / 32.0) - (norms + norm_row[...])).astype(BF16)
        kmat[rows, :] = kern
        images = lax.dot_general(vec_low[...], kern, NT, preferred_element_type=F32)
        for r in range(2):
            for j in range(2):
                im_src[i // 2, 4 * r + 2 * (i % 2) + j] = images[16 * r:16 * r + 16, 128 * j:128 * j + 128]

    kernel_step(0)
    kernel_step(1)

    scatter_count = 8 - jnp.where(rs_own, 1, 0)
    result_count = jnp.where(last, 7, 16 - jnp.where(out_own, 1, 0))
    place_count = jnp.where(diag, 3 + 4 * (3 - k), jnp.where(first_pair, 4, 1)) + jnp.where(below, 8, 0)
    pl.semaphore_wait(barrier, 7 + 3 + scatter_count + result_count + place_count)

    def send_images(half):
        for n, d in enumerate(AROUND):
            i = (y + d) % 8
            send(im_src.at[half, i], im_rs.at[half, y], S_IR + 7 * half + n, R_IR + half, device(x, i, z, c),
                 like=lambda: im_src.at[0, 0])
        stay(im_src.at[half, y], im_rs.at[half, y], R_IR + half)

    def phase_images():
        send_images(0)
        phase_factor()
        kernel_step(2)
        kernel_step(3)
        send_images(1)

    my_rows = pl.ds(pl.multiple_of(c * 256, 256), 256)
    keep = pl.ds(pl.multiple_of(c * 1024, 1024), 1024)
    give = pl.ds(pl.multiple_of((1 - c) * 1024, 1024), 1024)
    partner = device(x, y, z, 1 - c)

    def phase_factor():
        send(factor.at[:, give], fraw.at[my_rows, :], S_FX, R_FX, partner, works, lambda: fraw.at[0:256, :])

        @pl.when(works)
        def _():
            stay(factor.at[:, keep], fraw.at[my_rows, :], R_FX)

    def phase_split():
        @pl.when(works)
        def _():
            arrived(fraw, R_FX)
            raw = fraw[...]
            high = raw.astype(BF16)
            fhigh[...] = high
            flow[...] = (raw - high.astype(F32)).astype(BF16)

    def eight(buf, *lead):
        v = [buf[(*lead, i)] for i in range(8)]
        return ((v[0] + v[1]) + (v[2] + v[3])) + ((v[4] + v[5]) + (v[6] + v[7]))

    def phase_rounded():
        for half in range(2):
            arrived(im_rs.at[half], R_IR + half)
            ag_src[half] = (eight(im_rs, half) / 65536.0).astype(BF16).astype(F32)
            for n, d in enumerate(AROUND):
                send(ag_src.at[half], im_ag.at[half, y], S_IG + 7 * half + n, R_IG + half,
                     device(x, (y + d) % 8, z, c))
            stay(ag_src.at[half], im_ag.at[half, y], R_IG + half)

    def piece(b):
        zb, hb, cb = (z + b // 4) % 2, (h + b // 2 % 2) % 2, (c + b % 2) % 2
        return 4 * zb + 2 * hb + cb, (2 * k + hb, 4 * h + 2 * c + zb, cb)

    def scatter(src, dst, s, r, to, own, away, bits):
        for b in bits:
            g, place = piece(b)
            send(src.at[g], dst, s + b, r, device(to, *place), None if b else away, lambda: src.at[0])
            if not b:
                pl.when(own)(lambda: stay(src.at[g], dst, r))

    def phase_totals():
        for half in range(2):
            arrived(im_ag.at[half], R_IG + half)
            for i in range(8):
                im_low[16 * (i // 4):16 * (i // 4) + 16, 512 * half + 128 * (i % 4):512 * half + 128 * (i % 4) + 128] = (
                    im_ag[half, i].astype(BF16))
            rows = pl.ds(512 * half, 512)
            low = im_low[:, 512 * half:512 * half + 512]
            theirs = lax.dot_general(low, kmat[rows, give], NN, preferred_element_type=F32)
            if half == 0:
                t_src[...] = theirs
                t_keep[...] = lax.dot_general(low, kmat[rows, keep], NN, preferred_element_type=F32)
        t_src[...] += theirs
        send(t_src, t_rc, S_TC, R_TC, partner)
        mine = t_keep[...] + lax.dot_general(low, kmat[rows, keep], NN, preferred_element_type=F32)
        arrived(t_rc, R_TC)
        mine = mine + t_rc[...]
        for i in range(8):
            rs_src[i] = mine[:, i * 128:(i + 1) * 128]
        scatter(rs_src, rs_t.at[z], S_RT, R_RT, x, rs_own, rs_away, (7, 6, 5, 4, 3, 2, 1, 0))

    def phase_across():
        arrived(rs_t, R_RT)
        x_src[...] = eight(rs_t)
        send(x_src, x_buf.at[(x - k + 3) % 4], S_X, R_X, device(k, y, z, c), off_diag & later_pair)

        @pl.when(first_pair)
        def _():
            first = len(pending)
            spot = x_quad.at[x, 2 * h + c]
            for n in (3, 2, 1):
                send(x_src, spot, S_G + n, R_XQ, device(0, (h + n // 2) % 2, z, (c + n % 2) % 2))
            send(x_src, spot, S_G, R_XQ, device(0, y, z, c), off_diag)
            pl.when(diag)(lambda: stay(x_src, spot, R_XQ))
            nested(first, first_pair)

    def phase_residual():
        @pl.when(diag & first_pair)
        def _():
            arrived(x_quad, R_XQ)
            for i in range(4):
                inp[i] = (x_quad[0, i] + x_quad[1, i]) + (x_quad[2, i] + x_quad[3, i])

        @pl.when(later_diag)
        def _():
            first = len(pending)
            arrived(x_buf, R_X)
            s_src[...] = (x_src[...] + x_buf[0]) + (x_buf[1] + x_buf[2])
            for j in range(3):
                @pl.when(j < k)
                def _():
                    arrived(rs_ab.at[j], R_AB + j)
                    s_src[...] -= eight(rs_ab, j)
            for n in (3, 2, 1):
                send(s_src, inp.at[2 * h + c], S_G + n, R_IN,
                     device(x, 2 * k + (h + n // 2) % 2, z, (c + n % 2) % 2))
            stay(s_src, inp.at[2 * h + c], R_IN)
            nested(first, later_diag)

    def phase_product():
        @pl.when(works)
        def _():
            first = len(pending)
            pl.when(fed)(lambda: arrived(inp, R_IN))
            v = jnp.concatenate([inp[i] for i in range(4)], axis=1)
            high = v.astype(BF16)
            both = jnp.concatenate([high, (v - high.astype(F32)).astype(BF16)], axis=0)
            far = jnp.where(plain, (z // 4 + 1) % 2, (z + 1) % 2) * 4
            for own_half in range(2):
                start = far + own_half * (4 - 2 * far)
                cols = pl.ds(pl.multiple_of(start * 128, 512), 512)
                prod = lax.dot_general(both, fhigh[:, cols], NN, preferred_element_type=F32)
                rest = lax.dot_general(high, flow[:, cols], NN, preferred_element_type=F32)
                part = prod[0:32] + (prod[32:64] + rest)
                for i in range(4):
                    ab_src[start + i] = part[:, i * 128:(i + 1) * 128]

                @pl.when(plain)
                def _():
                    inside = len(pending)
                    for n in range(4):
                        g = start + (z + 2 + n) % 4
                        if own_half and n == 2:
                            stay(ab_src.at[g], rs_ab.at[x, z], R_AB + x)
                        else:
                            send(ab_src.at[g], rs_ab.at[x, z], S_RA + 4 * own_half + n, R_AB + x,
                                 device(x, y, g, c), None, lambda: ab_src.at[0])
                    nested(inside, plain)

                @pl.when(dealt)
                def _():
                    inside = len(pending)
                    bits = (3, 2, 1, 0) if own_half else (7, 6, 5, 4)
                    scatter(ab_src, rs_ab.at[x, z], S_RA, R_AB + x, k, ab_own, ab_away, bits)
                    nested(inside, dealt)
            nested(first, works)

    def phase_solved():
        @pl.when(diag)
        def _():
            first = len(pending)
            arrived(rs_ab.at[k], R_AB + k)
            u_src[...] = eight(rs_ab, k)
            for j in range(3):
                for n in range(4):
                    send(u_src, inp.at[2 * h + c], S_B + 4 * j + n, R_IN,
                         device(x, (2 * (k + 1 + j) + n // 2) % 8, z, n % 2), more[j])
            for n in range(3):
                send(u_src, u_src, S_O1 + n, R_O1, device((x + 1 + n) % 4, y, z, c))
            nested(first, diag)

        @pl.when(jnp.logical_not(diag))
        def _():
            arrived(u_src, R_O1)

    def phase_results():
        before = pending[:]
        del pending[:]

        @pl.when(not_last)
        def _():
            first = len(pending)
            slot = (z % 4) * 4 + 2 * h + c
            for n, d in enumerate(AROUND):
                for e in range(2):
                    zt = (z + d) % 8
                    send(u_src, o_buf.at[slot], S_O2 + 2 * n + e, R_O2, device(x, 2 * k + z // 4, zt, (c + e) % 2))
            send(u_src, o_buf.at[slot], S_O2 + 14, R_O2, device(x, 2 * k + z // 4, z, 1 - c))
            send(u_src, o_buf.at[slot], S_O2 + 15, R_O2, device(x, 2 * k + z // 4, z, c), out_away)
            pl.when(out_own)(lambda: stay(u_src, o_buf.at[slot], R_O2))
            nested(first, not_last)

        @pl.when(last)
        def _():
            first = len(pending)
            slot = c * 8 + z
            for n, d in enumerate(AROUND):
                send(u_src, o_buf.at[slot], S_O2 + n, R_O2, device(x, y, (z + d) % 8, c))
            stay(u_src, o_buf.at[slot], R_O2)
            nested(first, last)

        for wait in before:
            wait()

        def write(start):
            for i in range(8):
                out_vm[:, pl.ds(pl.multiple_of((start + i) * 128, 128), 128)] = o_buf[start + i]
            cols = pl.ds(pl.multiple_of(start * 128, 1024), 1024)
            pltpu.make_async_copy(out_vm.at[:, cols], out.at[:, cols], rsem.at[L_O]).start()

        @pl.when(not_last)
        def _():
            arrived(o_buf, R_O2)
            write(0)
            write(8)

        @pl.when(last)
        def _():
            first = len(pending)
            mine = o_buf.at[pl.ds(c * 8, 8)]
            arrived(mine, R_O2)
            send(mine, mine, S_O3, R_O3, partner, None, lambda: o_buf.at[0:8])
            write(c * 8)
            nested(first, last)
        for wait in pending[:-1]:
            wait()

        @pl.when(last)
        def _():
            arrived(o_buf.at[pl.ds(8 - c * 8, 8)], R_O3)
            write(8 - c * 8)
        pending[-1]()
        arrived(out_vm, L_O)

    phases = (phase_images, phase_rounded, phase_totals, phase_across, phase_split, phase_residual,
              phase_product, phase_solved, phase_results)
    for phase in phases:
        phase()


def body(points, centres, vector, factor):
    def piece(*lead):
        return pltpu.VMEM((*lead, 32, 128), F32)

    any_space = pl.BlockSpec(memory_space=pl.ANY)
    return pl.pallas_call(
        sweep_kernel,
        out_shape=jax.ShapeDtypeStruct((32, 2048), F32),
        in_specs=[any_space] * 4,
        out_specs=any_space,
        scratch_shapes=[
            pltpu.VMEM((1024, 512), BF16), pltpu.VMEM((2048, 512), BF16), pltpu.VMEM((32, 2048), F32),
            pltpu.VMEM((32, 2048), BF16), pltpu.VMEM((1, 2048), F32), pltpu.VMEM((1024, 2048), BF16),
            pltpu.VMEM((512, 1024), F32), pltpu.VMEM((512, 1024), BF16), pltpu.VMEM((512, 1024), BF16),
            pltpu.VMEM((2, 8, 16, 128), F32), pltpu.VMEM((2, 8, 16, 128), F32), pltpu.VMEM((2, 16, 128), F32),
            pltpu.VMEM((2, 8, 16, 128), F32), pltpu.VMEM((32, 1024), BF16), pltpu.VMEM((32, 1024), F32),
            pltpu.VMEM((32, 1024), F32), pltpu.VMEM((32, 1024), F32), piece(8), piece(8), piece(), piece(3),
            piece(), piece(4), piece(8), piece(4, 8), piece(), piece(16), piece(4, 4), pltpu.VMEM((32, 2048), F32),
            pltpu.SemaphoreType.DMA((S_END,)), pltpu.SemaphoreType.DMA((R_END,)),
        ],
        compiler_params=pltpu.CompilerParams(
            collective_id=0, has_side_effects=True, vmem_limit_bytes=60 * 2**20),
        cost_estimate=pl.CostEstimate(
            flops=2 * 1024 * 2048 * 512, bytes_accessed=6 * 2**20, transcendentals=1024 * 2048),
    )(points, centres, vector, factor)


def solution(mesh):
    placed = (P("pts", None), P("ctr", None), P(None, "ctr"), P("pts", "ctr"))
    return jax.shard_map(
        body, mesh=mesh, in_specs=placed, out_specs=P(None, "ctr"), check_vma=False
    )
```

```python
import jax
import jax.numpy as jnp
from jax import lax
from jax.experimental import pallas as pl
from jax.experimental.pallas import tpu as pltpu
from jax.sharding import PartitionSpec as P

F32, BF16 = jnp.float32, jnp.bfloat16
MESH = pl.DeviceIdType.MESH
NN = (((1,), (0,)), ((), ()))
NT = (((1,), (1,)), ((), ()))
PT = 256
AROUND = (4, 3, 5, 2, 6, 1, 7)
S_IR, S_IG, S_TC, S_FX, S_RT, S_X, S_G, S_RA, S_B, S_O1, S_O2, S_O3, S_END = (
    0, 14, 28, 29, 30, 38, 42, 46, 54, 66, 70, 86, 87)
(R_IR, R_IG, R_TC, R_FX, R_RT, R_X, R_IN, R_AB, R_O1, R_O2, R_O3, R_XQ, L_C, L_P, L_V, L_O, R_END) = (
    0, 2, 4, 5, 6, 7, 8, 9, 13, 14, 15, 16, 17, 18, 19, 20, 21)


def device(x, y, z, c):
    return ((x * 8 + z) * 2 + c, y)


def sweep_kernel(
    points, centres, vector, factor, out,
    pts, cen, vec, vec_low, norm_row, kmat, fraw, fhigh, flow,
    im_src, im_rs, ag_src, im_ag, im_low, t_keep, t_src, t_rc, rs_src, rs_t, x_src, x_buf,
    s_src, inp, ab_src, rs_ab, u_src, o_buf, x_quad, out_vm, ssem, rsem,
):
    p, y = lax.axis_index("pts"), lax.axis_index("ctr")
    x, z, c = p // 16, (p // 2) % 8, p % 2
    k, h = y // 2, y % 2
    diag, works, below, last = x == k, x <= k, x < k, k == 3
    first_pair = k == 0

    pending = []

    def send(src, dst, s, r, dev, when=None, like=None):
        def start():
            pltpu.make_async_remote_copy(
                src_ref=src, dst_ref=dst, send_sem=ssem.at[s], recv_sem=rsem.at[r],
                device_id=dev, device_id_type=MESH).start()

        def sent():
            buf = src if like is None else like()
            pltpu.make_async_copy(buf, buf, ssem.at[s]).wait()
        if when is None:
            start()
            pending.append(sent)
        else:
            pl.when(when)(start)
            pending.append(lambda: pl.when(when)(sent))

    def nested(first, when):
        inner = pending[first:]
        del pending[first:]

        def waits():
            for wait in inner:
                wait()
        pending.append(lambda: pl.when(when)(waits))

    def stay(src, dst, r):
        pltpu.make_async_copy(src, dst, rsem.at[r]).start()

    def arrived(buf, r):
        pltpu.make_async_copy(buf, buf, rsem.at[r]).wait()

    def each(n, f):
        def step(i, carry):
            f(i)
            return carry
        lax.fori_loop(0, n, step, 0)

    load_c = pltpu.make_async_copy(centres, cen, rsem.at[L_C])
    load_p = pltpu.make_async_copy(points, pts, rsem.at[L_P])
    load_v = pltpu.make_async_copy(vector, vec, rsem.at[L_V])
    load_c.start()
    load_p.start()
    load_v.start()

    barrier = pltpu.get_barrier_semaphore()

    def greet(dev):
        pl.semaphore_signal(barrier, inc=1, device_id=dev, device_id_type=MESH)

    each(7, lambda i: greet(device(x, (y + 1 + i) % 8, z, c)))
    each(3, lambda i: greet(device(x, 2 * k + (h + (i + 1) // 2) % 2, z, (c + (i + 1) % 2) % 2)))
    rs_own = z // 2 == 2 * h + c
    rs_y, rs_c = 2 * k + z // 4, (z // 2) % 2

    def greet_rs(i):
        @pl.when(jnp.logical_not(rs_own & (i == z)))
        def _():
            greet(device(x, rs_y, i, rs_c))
    each(8, greet_rs)

    def greet_out(i):
        dev = (2 * k + i // 2 % 2, 4 * h + i // 4, i % 2)

        @pl.when(jnp.logical_not((dev[0] == y) & (dev[1] == z) & (dev[2] == c)))
        def _():
            greet(device(x, *dev))
    pl.when(jnp.logical_not(last))(lambda: each(16, greet_out))
    pl.when(last)(lambda: each(7, lambda i: greet(device(x, y, (z + 1 + i) % 8, c))))
    out_own = z // 4 == h
    later_pair = jnp.logical_not(first_pair)
    fed = jnp.logical_not(diag & first_pair)
    later_diag = diag & later_pair
    rs_away, out_away = jnp.logical_not(rs_own), jnp.logical_not(out_own)
    off_diag, not_last = jnp.logical_not(diag), jnp.logical_not(last)
    plain = diag & last
    dealt = works & jnp.logical_not(plain)
    ab_own = rs_own & diag
    ab_away = jnp.logical_not(ab_own)
    more = [k + 1 + j <= 3 for j in range(3)]

    @pl.when(diag)
    def _():
        @pl.when(first_pair)
        def _():
            each(12, lambda i: greet(device(1 + i // 4, i // 2 % 2, z, i % 2)))

        @pl.when(jnp.logical_not(first_pair))
        def _():
            each(3, lambda i: greet(device((x + 1 + i) % 4, y, z, c)))
        each(8 * k, lambda i: greet(device(i // 8, rs_y, i % 8, rs_c)))

    @pl.when(jnp.logical_not(diag))
    def _():
        greet(device(k, y, z, c))

    @pl.when(below)
    def _():
        each(4, lambda i: greet(device(x, 2 * x + i // 2, z, i % 2)))

    load_c.wait()
    squares = jnp.square(cen[...].astype(F32))
    folded = (squares[:, 0:128] + squares[:, 128:256]) + (squares[:, 256:384] + squares[:, 384:512])
    norm_row[...] = jnp.sum(folded.T, axis=0, keepdims=True) * (1.0 / 64.0)
    load_p.wait()
    load_v.wait()
    vec_low[...] = vec[...].astype(BF16)

    def kernel_step(i):
        rows = pl.ds(i * PT, PT)
        pt = pts[rows, :]
        prods = lax.dot_general(pt, cen[...], NT, preferred_element_type=F32)
        norms = jnp.sum(jnp.square(pt.astype(F32)), axis=1, keepdims=True) * (1.0 / 64.0)
        kern = jnp.exp(prods * (1.0 / 32.0) - (norms + norm_row[...])).astype(BF16)
        kmat[rows, :] = kern
        images = lax.dot_general(vec_low[...], kern, NT, preferred_element_type=F32)
        for r in range(2):
            for j in range(2):
                im_src[i // 2, 4 * r + 2 * (i % 2) + j] = images[16 * r:16 * r + 16, 128 * j:128 * j + 128]

    kernel_step(0)
    kernel_step(1)

    scatter_count = 8 - jnp.where(rs_own, 1, 0)
    result_count = jnp.where(last, 7, 16 - jnp.where(out_own, 1, 0))
    place_count = jnp.where(diag, 3 + 4 * (3 - k), jnp.where(first_pair, 4, 1)) + jnp.where(below, 8, 0)
    pl.semaphore_wait(barrier, 7 + 3 + scatter_count + result_count + place_count)

    def send_images(half):
        for n, d in enumerate(AROUND):
            i = (y + d) % 8
            send(im_src.at[half, i], im_rs.at[half, y], S_IR + 7 * half + n, R_IR + half, device(x, i, z, c),
                 like=lambda: im_src.at[0, 0])
        stay(im_src.at[half, y], im_rs.at[half, y], R_IR + half)

    def phase_images():
        send_images(0)
        phase_factor()
        kernel_step(2)
        kernel_step(3)
        send_images(1)

    my_rows = pl.ds(pl.multiple_of(c * 256, 256), 256)
    keep = pl.ds(pl.multiple_of(c * 1024, 1024), 1024)
    give = pl.ds(pl.multiple_of((1 - c) * 1024, 1024), 1024)
    partner = device(x, y, z, 1 - c)

    def phase_factor():
        send(factor.at[:, give], fraw.at[my_rows, :], S_FX, R_FX, partner, works, lambda: fraw.at[0:256, :])

        @pl.when(works)
        def _():
            stay(factor.at[:, keep], fraw.at[my_rows, :], R_FX)

    def phase_split():
        @pl.when(works)
        def _():
            arrived(fraw, R_FX)
            raw = fraw[...]
            high = raw.astype(BF16)
            fhigh[...] = high
            flow[...] = (raw - high.astype(F32)).astype(BF16)

    def eight(buf, *lead):
        v = [buf[(*lead, i)] for i in range(8)]
        return ((v[0] + v[1]) + (v[2] + v[3])) + ((v[4] + v[5]) + (v[6] + v[7]))

    def phase_rounded():
        for half in range(2):
            arrived(im_rs.at[half], R_IR + half)
            ag_src[half] = (eight(im_rs, half) / 65536.0).astype(BF16).astype(F32)
            for n, d in enumerate(AROUND):
                send(ag_src.at[half], im_ag.at[half, y], S_IG + 7 * half + n, R_IG + half,
                     device(x, (y + d) % 8, z, c))
            stay(ag_src.at[half], im_ag.at[half, y], R_IG + half)

    def piece(b):
        zb, hb, cb = (z + b // 4) % 2, (h + b // 2 % 2) % 2, (c + b % 2) % 2
        return 4 * zb + 2 * hb + cb, (2 * k + hb, 4 * h + 2 * c + zb, cb)

    def scatter(src, dst, s, r, to, own, away, bits):
        for b in bits:
            g, place = piece(b)
            send(src.at[g], dst, s + b, r, device(to, *place), None if b else away, lambda: src.at[0])
            if not b:
                pl.when(own)(lambda: stay(src.at[g], dst, r))

    def phase_totals():
        for half in range(2):
            arrived(im_ag.at[half], R_IG + half)
            for i in range(8):
                im_low[16 * (i // 4):16 * (i // 4) + 16, 512 * half + 128 * (i % 4):512 * half + 128 * (i % 4) + 128] = (
                    im_ag[half, i].astype(BF16))
            rows = pl.ds(512 * half, 512)
            low = im_low[:, 512 * half:512 * half + 512]
            theirs = lax.dot_general(low, kmat[rows, give], NN, preferred_element_type=F32)
            if half == 0:
                t_src[...] = theirs
                t_keep[...] = lax.dot_general(low, kmat[rows, keep], NN, preferred_element_type=F32)
        t_src[...] += theirs
        send(t_src, t_rc, S_TC, R_TC, partner)
        mine = t_keep[...] + lax.dot_general(low, kmat[rows, keep], NN, preferred_element_type=F32)
        arrived(t_rc, R_TC)
        mine = mine + t_rc[...]
        for i in range(8):
            rs_src[i] = mine[:, i * 128:(i + 1) * 128]
        scatter(rs_src, rs_t.at[z], S_RT, R_RT, x, rs_own, rs_away, (7, 6, 5, 4, 3, 2, 1, 0))

    def phase_across():
        arrived(rs_t, R_RT)
        x_src[...] = eight(rs_t)
        send(x_src, x_buf.at[(x - k + 3) % 4], S_X, R_X, device(k, y, z, c), off_diag & later_pair)

        @pl.when(first_pair)
        def _():
            first = len(pending)
            spot = x_quad.at[x, 2 * h + c]
            for n in (3, 2, 1):
                send(x_src, spot, S_G + n, R_XQ, device(0, (h + n // 2) % 2, z, (c + n % 2) % 2))
            send(x_src, spot, S_G, R_XQ, device(0, y, z, c), off_diag)
            pl.when(diag)(lambda: stay(x_src, spot, R_XQ))
            nested(first, first_pair)

    def phase_residual():
        @pl.when(diag & first_pair)
        def _():
            arrived(x_quad, R_XQ)
            for i in range(4):
                inp[i] = (x_quad[0, i] + x_quad[1, i]) + (x_quad[2, i] + x_quad[3, i])

        @pl.when(later_diag)
        def _():
            first = len(pending)
            arrived(x_buf, R_X)
            s_src[...] = (x_src[...] + x_buf[0]) + (x_buf[1] + x_buf[2])
            for j in range(3):
                @pl.when(j < k)
                def _():
                    arrived(rs_ab.at[j], R_AB + j)
                    s_src[...] -= eight(rs_ab, j)
            for n in (3, 2, 1):
                send(s_src, inp.at[2 * h + c], S_G + n, R_IN,
                     device(x, 2 * k + (h + n // 2) % 2, z, (c + n % 2) % 2))
            stay(s_src, inp.at[2 * h + c], R_IN)
            nested(first, later_diag)

    def phase_product():
        @pl.when(works)
        def _():
            first = len(pending)
            pl.when(fed)(lambda: arrived(inp, R_IN))
            v = jnp.concatenate([inp[i] for i in range(4)], axis=1)
            high = v.astype(BF16)
            both = jnp.concatenate([high, (v - high.astype(F32)).astype(BF16)], axis=0)
            for i in range(4):
                far = (i < 2) + 0
                along = (z // 4 + far) % 2 * 4 + (2 * i if far else (z // 2 + 1 - i % 2) % 2 * 2)
                dealt_out = (z + far) % 2 * 4 + (h + 1 - i % 2) % 2 * 2
                start = jnp.where(plain, along, dealt_out)
                cols = pl.ds(pl.multiple_of(start * 128, 256), 256)
                prod = lax.dot_general(both, fhigh[:, cols], NN, preferred_element_type=F32)
                rest = lax.dot_general(high, flow[:, cols], NN, preferred_element_type=F32)
                part = prod[0:32] + (prod[32:64] + rest)
                ab_src[start] = part[:, 0:128]
                ab_src[start + 1] = part[:, 128:256]

                @pl.when(plain)
                def _():
                    inside = len(pending)
                    for n in range(2):
                        g = along + (z + 1 + n) % 2
                        if i == 3 and n == 1:
                            stay(ab_src.at[g], rs_ab.at[x, z], R_AB + x)
                        else:
                            send(ab_src.at[g], rs_ab.at[x, z], S_RA + 2 * i + n, R_AB + x,
                                 device(x, y, g, c), None, lambda: ab_src.at[0])
                    nested(inside, plain)

                @pl.when(dealt)
                def _():
                    inside = len(pending)
                    scatter(ab_src, rs_ab.at[x, z], S_RA, R_AB + x, k, ab_own, ab_away, (7 - 2 * i, 6 - 2 * i))
                    nested(inside, dealt)
            nested(first, works)

    def phase_solved():
        @pl.when(diag)
        def _():
            first = len(pending)
            arrived(rs_ab.at[k], R_AB + k)
            u_src[...] = eight(rs_ab, k)
            for j in range(3):
                for n in range(4):
                    send(u_src, inp.at[2 * h + c], S_B + 4 * j + n, R_IN,
                         device(x, (2 * (k + 1 + j) + n // 2) % 8, z, n % 2), more[j])
            for n in range(3):
                send(u_src, u_src, S_O1 + n, R_O1, device((x + 1 + n) % 4, y, z, c))
            nested(first, diag)

        @pl.when(jnp.logical_not(diag))
        def _():
            arrived(u_src, R_O1)

    def phase_results():
        before = pending[:]
        del pending[:]

        @pl.when(not_last)
        def _():
            first = len(pending)
            slot = (z % 4) * 4 + 2 * h + c
            for n, d in enumerate(AROUND):
                for e in range(2):
                    zt = (z + d) % 8
                    send(u_src, o_buf.at[slot], S_O2 + 2 * n + e, R_O2, device(x, 2 * k + z // 4, zt, (c + e) % 2))
            send(u_src, o_buf.at[slot], S_O2 + 14, R_O2, device(x, 2 * k + z // 4, z, 1 - c))
            send(u_src, o_buf.at[slot], S_O2 + 15, R_O2, device(x, 2 * k + z // 4, z, c), out_away)
            pl.when(out_own)(lambda: stay(u_src, o_buf.at[slot], R_O2))
            nested(first, not_last)

        @pl.when(last)
        def _():
            first = len(pending)
            slot = c * 8 + z
            for n, d in enumerate(AROUND):
                send(u_src, o_buf.at[slot], S_O2 + n, R_O2, device(x, y, (z + d) % 8, c))
            stay(u_src, o_buf.at[slot], R_O2)
            nested(first, last)

        for wait in before:
            wait()

        def write(start):
            for i in range(8):
                out_vm[:, pl.ds(pl.multiple_of((start + i) * 128, 128), 128)] = o_buf[start + i]
            cols = pl.ds(pl.multiple_of(start * 128, 1024), 1024)
            pltpu.make_async_copy(out_vm.at[:, cols], out.at[:, cols], rsem.at[L_O]).start()

        @pl.when(not_last)
        def _():
            arrived(o_buf, R_O2)
            write(0)
            write(8)

        @pl.when(last)
        def _():
            first = len(pending)
            mine = o_buf.at[pl.ds(c * 8, 8)]
            arrived(mine, R_O2)
            send(mine, mine, S_O3, R_O3, partner, None, lambda: o_buf.at[0:8])
            write(c * 8)
            nested(first, last)
        for wait in pending[:-1]:
            wait()

        @pl.when(last)
        def _():
            arrived(o_buf.at[pl.ds(8 - c * 8, 8)], R_O3)
            write(8 - c * 8)
        pending[-1]()
        arrived(out_vm, L_O)

    phases = (phase_images, phase_rounded, phase_totals, phase_across, phase_split, phase_residual,
              phase_product, phase_solved, phase_results)
    for phase in phases:
        phase()


def body(points, centres, vector, factor):
    def piece(*lead):
        return pltpu.VMEM((*lead, 32, 128), F32)

    any_space = pl.BlockSpec(memory_space=pl.ANY)
    return pl.pallas_call(
        sweep_kernel,
        out_shape=jax.ShapeDtypeStruct((32, 2048), F32),
        in_specs=[any_space] * 4,
        out_specs=any_space,
        scratch_shapes=[
            pltpu.VMEM((1024, 512), BF16), pltpu.VMEM((2048, 512), BF16), pltpu.VMEM((32, 2048), F32),
            pltpu.VMEM((32, 2048), BF16), pltpu.VMEM((1, 2048), F32), pltpu.VMEM((1024, 2048), BF16),
            pltpu.VMEM((512, 1024), F32), pltpu.VMEM((512, 1024), BF16), pltpu.VMEM((512, 1024), BF16),
            pltpu.VMEM((2, 8, 16, 128), F32), pltpu.VMEM((2, 8, 16, 128), F32), pltpu.VMEM((2, 16, 128), F32),
            pltpu.VMEM((2, 8, 16, 128), F32), pltpu.VMEM((32, 1024), BF16), pltpu.VMEM((32, 1024), F32),
            pltpu.VMEM((32, 1024), F32), pltpu.VMEM((32, 1024), F32), piece(8), piece(8), piece(), piece(3),
            piece(), piece(4), piece(8), piece(4, 8), piece(), piece(16), piece(4, 4), pltpu.VMEM((32, 2048), F32),
            pltpu.SemaphoreType.DMA((S_END,)), pltpu.SemaphoreType.DMA((R_END,)),
        ],
        compiler_params=pltpu.CompilerParams(
            collective_id=0, has_side_effects=True, vmem_limit_bytes=60 * 2**20),
        cost_estimate=pl.CostEstimate(
            flops=2 * 1024 * 2048 * 512, bytes_accessed=6 * 2**20, transcendentals=1024 * 2048),
    )(points, centres, vector, factor)


def solution(mesh):
    placed = (P("pts", None), P("ctr", None), P(None, "ctr"), P("pts", "ctr"))
    return jax.shard_map(
        body, mesh=mesh, in_specs=placed, out_specs=P(None, "ctr"), check_vma=False
    )
```
